32 devices in a mesh: grp: 2 (over x), tile: 16 (over z, y, core).
Axes of the slice: x: 2, y: 2, z: 4, core: 2. Of those that a mesh axis runs over, the one named last changes fastest.
Arguments:
- latent: float32 [32, 1024, 128], P(None, ('grp', 'tile')), parts along dimension 1, may hold values from -6 to 6
- observed: float32 [32, 1024, 128], P(None, ('grp', 'tile')), parts along dimension 1, may hold values from -6 to 6
- noise: float32 [32, 1024, 128], P(None, ('grp', 'tile')), parts along dimension 1, may hold values from -6 to 6
- cloudy: int32 [128], P(('grp', 'tile')), parts along dimension 0, may hold values from 0 to 1, as said below
- timestep: int32 [2], P('grp'), parts along dimension 0, may hold values from 200 to 800
- pos_embed: bfloat16 [256, 2048], replicated, may hold values from -3 to 3
- embed_w: bfloat16 [128, 2048], replicated, may hold values from -0.5 to 0.5
- mod_w: bfloat16 [256, 6144], P(None, 'tile'), may hold values from -0.375 to 0.375
- wq: bfloat16 [2048, 1024], P('tile')
- wk: bfloat16 [2048, 1024], P('tile')
- wv: bfloat16 [2048, 1024], P('tile'), may hold values from -0.125 to 0.125
- wo: bfloat16 [1024, 2048], P(None, 'tile'), may hold values from -0.1875 to 0.1875
- q_gain: float32 [128], replicated, may hold values from 0.6 to 4.2
- k_gain: float32 [128], replicated, may hold values from 0.6 to 4.2
- out_w: bfloat16 [2048, 128], replicated, may hold values from -0.125 to 0.125
- conv_w: float32 [9, 32, 32], replicated, may hold values from -0.375 to 0.375
Outputs:
- estimate: float32 [32, 1024, 128], P(None, ('grp', 'tile')), parts along dimension 1
- next_latent: float32 [32, 1024, 128], P(None, ('grp', 'tile')), parts along dimension 1
The draws below stay inside these ranges and needn't reach their ends.
There are 2 independent parts, one for each index of `grp`. The reference program is written for one: setup_inputs(seed, part) draws one part's arguments, and reference() takes and returns one part's arrays. A program takes and returns all parts, laid end to end along the dimension named above; an argument that names none is the same for every part. Nothing has to cross between parts.
Inputs may be any that keep to these rules, and one draw needn't show every extreme that they name: Exactly 16 tiles of a part are cloudy; each band of 4 tiles holds at most 3 of them, and some band holds exactly 3.
All inputs are finite; a program needn't handle non-finite values.
Results may differ from the reference program's by a relative error of at most 0.0033.
Values may be sent and summed in bfloat16 or wider, within the bound.
A program may use at most 128 MiB of HBM per device.

```python
import math
import jax
import jax.numpy as jnp
from jax import lax

D = 2048
HD = 128
INNER = 1024
FREQ = 256
LATC = 32
PATCH = 2
PV = 128
TSIDE = 16
TT = 256
TPX = 32
TILES_DEV = 4
TSTEPS = 1000
STRIDE = 20
OWNERS = 16
TILES = 64
HL = 512
WL = 128
N_TILE = 16


def draw_cloudy(key, part):
    owners = TILES // TILES_DEV
    groups = owners // 4
    patterns = jnp.array([[3, 1, 0, 0], [2, 1, 1, 0], [2, 2, 0, 0], [1, 1, 1, 1]], jnp.int32)
    picks = jax.random.randint(jax.random.fold_in(key, 1), (groups,), 0, 4)
    picks = picks.at[0].set(0)
    group_counts = patterns[picks]
    scores = jax.random.randint(jax.random.fold_in(key, 2), (groups, 4), 0, 1 << 20) * 4 + jnp.arange(4, dtype=jnp.int32)[None, :]
    order = jnp.argsort(scores, axis=1)
    group_counts = jnp.take_along_axis(group_counts, order, axis=1)
    counts = jax.random.permutation(jax.random.fold_in(key, 3), group_counts.reshape(owners))
    tile_scores = jax.random.randint(jax.random.fold_in(key, 4), (owners, TILES_DEV), 0, 1 << 20) * TILES_DEV + jnp.arange(TILES_DEV, dtype=jnp.int32)[None, :]
    ranks = jnp.argsort(jnp.argsort(tile_scores, axis=1), axis=1)
    flags = (ranks < counts[:, None]).astype(jnp.int32)
    return flags.reshape(TILES)


def query_key_pair(key):
    first = jax.random.normal(jax.random.fold_in(key, 101), (D, INNER), jnp.float32)
    other = jax.random.normal(jax.random.fold_in(key, 102), (D, INNER), jnp.float32)
    first = jnp.clip(first, -5.0, 5.0)
    other = jnp.clip(other, -5.0, 5.0)
    second = other
    return (first * D ** (-0.5), second * D ** (-0.5))


def draw_wq(key, part):
    return query_key_pair(key)[0].astype(jnp.bfloat16)


def draw_wk(key, part):
    return query_key_pair(key)[1].astype(jnp.bfloat16)


def gain_values(key, salt):
    inner_key = jax.random.fold_in(key, salt)
    values = jax.random.uniform(inner_key, (HD,), jnp.float32, 0.6, 1.8)
    return values


def draw_q_gain(key, part):
    return gain_values(key, 201)


def draw_k_gain(key, part):
    return gain_values(key, 202)


def levels(own_key, shape, cuts, low, high):
    factor_of = 1.0
    for position, blocks in cuts:
        heights = jax.random.uniform(jax.random.fold_in(jax.random.fold_in(own_key, 6), position), (blocks,), jnp.float32, low / len(cuts), high / len(cuts))
        factor_of = factor_of * jnp.repeat(jnp.exp(heights), shape[position] // blocks).reshape((-1,) + (1,) * (len(shape) - 1 - position))
    return factor_of


def normal_values(rng, shape, deviation, most, shards=(), kind=jnp.bfloat16):
    drawn = deviation * jax.random.normal(rng, shape, jnp.float32)
    if shards:
        drawn = drawn * levels(rng, shape, shards, -0.22, 0.18)
    return jnp.clip(drawn, -most, most).astype(kind)


def setup_inputs(seed: int = 0, part: int = 0) -> dict:
    keys = jax.random.split(jax.random.key(seed), 17)
    part_keys = jax.random.split(jax.random.fold_in(keys[16], part), 17)
    latent = normal_values(part_keys[0], (LATC, HL, WL), 1.0, 6.0, ((1, 16),), jnp.float32)
    observed = normal_values(part_keys[1], (LATC, HL, WL), 1.0, 6.0, ((1, 16),), jnp.float32)
    noise = normal_values(part_keys[2], (LATC, HL, WL), 1.0, 6.0, ((1, 16),), jnp.float32)
    cloudy = draw_cloudy(jax.random.fold_in(jax.random.fold_in(keys[16], part), 71), part)
    timestep = jax.random.randint(part_keys[4], (1,), 200, 801).astype(jnp.int32)
    pos_embed = normal_values(keys[5], (TT, D), 0.5, 3.0)
    embed_w = normal_values(keys[6], (PV, D), PV ** -0.5, 0.5)
    mod_w = normal_values(keys[7], (FREQ, 3 * D), FREQ ** -0.5, 0.375, ((1, 16),))
    wq = draw_wq(jax.random.fold_in(keys[16], 71), part)
    wk = draw_wk(jax.random.fold_in(keys[16], 71), part)
    wv = normal_values(keys[10], (D, INNER), D ** -0.5, 0.125, ((0, 16),))
    wo = normal_values(keys[11], (INNER, D), INNER ** -0.5, 0.1875, ((1, 16),))
    q_gain = draw_q_gain(jax.random.fold_in(keys[16], 71), part)
    k_gain = draw_k_gain(jax.random.fold_in(keys[16], 71), part)
    out_w = normal_values(keys[14], (D, PV), D ** -0.5, 0.125)
    conv_w = normal_values(keys[15], (9, LATC, LATC), (9 * LATC) ** -0.5, 0.375, (), jnp.float32)
    return dict(latent=latent, observed=observed, noise=noise, cloudy=cloudy, timestep=timestep, pos_embed=pos_embed, embed_w=embed_w, mod_w=mod_w, wq=wq, wk=wk, wv=wv, wo=wo, q_gain=q_gain, k_gain=k_gain, out_w=out_w, conv_w=conv_w)


def plan(step):
    theta = (step / TSTEPS + 0.008) / 1.008 * (math.pi / 2)
    return (jnp.cos(theta), jnp.sin(theta))

def time_features(step, width):
    half = width // 2
    freqs = jnp.exp(-math.log(10000.0) * jnp.arange(half, dtype=jnp.float32) / half)
    angles = step * freqs
    code = jnp.concatenate([jnp.cos(angles), jnp.sin(angles)])[None, :]
    return jax.nn.silu(code).astype(jnp.bfloat16)

def layer_norm(values):
    center = values - lax.optimization_barrier(jnp.mean(values, axis=-1, keepdims=True))
    spread = lax.optimization_barrier(jnp.mean(center * center, axis=-1, keepdims=True))
    return center * lax.rsqrt(spread + 1e-06)

def head_norm(proj, gain, count):
    shaped = proj.reshape(count, TT, -1, HD)
    scaled = shaped * lax.rsqrt(lax.optimization_barrier(jnp.mean(shaped * shaped, axis=-1, keepdims=True)) + 1e-06)
    return (scaled * gain).astype(jnp.bfloat16)

def denoise_tiles(chosen, embed_w, pos_embed, shift_vec, scale_vec, gate_vec, wq, wk, wv, wo, q_gain, k_gain, out_w):
    count = chosen.shape[0]
    row_count = count * TT
    flat = chosen.reshape(row_count, PV)
    hidden0 = jnp.dot(flat, embed_w, preferred_element_type=jnp.float32).reshape(count, TT, D)
    hidden0 = (hidden0 + pos_embed.astype(jnp.float32)[None]).reshape(row_count, D)
    modulated = (layer_norm(hidden0) * (1.0 + scale_vec) + shift_vec).astype(jnp.bfloat16)
    query_all = jnp.dot(modulated, wq, preferred_element_type=jnp.float32)
    key_all = jnp.dot(modulated, wk, preferred_element_type=jnp.float32)
    value_all = jnp.dot(modulated, wv, preferred_element_type=jnp.float32)
    query_norm = head_norm(query_all, q_gain, count).astype(jnp.float32)
    key_norm = head_norm(key_all, k_gain, count).astype(jnp.float32)
    value_half = value_all.reshape(count, TT, -1, HD).astype(jnp.bfloat16).astype(jnp.float32)
    scores = jnp.einsum('nqhd,nkhd->nhqk', query_norm, key_norm) * HD ** (-0.5)
    peak = lax.optimization_barrier(jnp.max(scores, axis=-1, keepdims=True))
    expo = jnp.exp(scores - peak)
    probs = (expo / lax.optimization_barrier(jnp.sum(expo, axis=-1, keepdims=True))).astype(jnp.bfloat16).astype(jnp.float32)
    mixed = jnp.einsum('nhqk,nkhd->nqhd', probs, value_half).astype(jnp.bfloat16).reshape(row_count, -1)
    attn_out = jnp.dot(mixed, wo, preferred_element_type=jnp.float32)
    hidden1 = hidden0 + gate_vec * attn_out
    final = layer_norm(hidden1).astype(jnp.bfloat16)
    eps_pred = jnp.dot(final, out_w, preferred_element_type=jnp.float32).astype(jnp.bfloat16)
    return eps_pred.reshape(count, TT, PV)

def all_tiles(scene_field):
    shaped = scene_field.reshape(LATC, N_TILE, TSIDE, PATCH, TILES_DEV, TSIDE, PATCH)
    return jnp.transpose(shaped, (1, 4, 2, 5, 3, 6, 0)).reshape(TILES, TT, PV)

def all_pixels(tiled):
    shaped = tiled.reshape(N_TILE, TILES_DEV, TSIDE, TSIDE, PATCH, PATCH, LATC)
    return jnp.transpose(shaped, (6, 0, 2, 4, 1, 3, 5)).reshape(LATC, HL, WL)

def reference(latent, observed, noise, cloudy, timestep, pos_embed, embed_w, mod_w, wq, wk, wv, wo, q_gain, k_gain, out_w, conv_w):
    step_now = timestep[0].astype(jnp.float32)
    cos_now, sin_now = plan(step_now)
    cos_prev, sin_prev = plan(step_now - STRIDE)
    time_code = time_features(step_now, FREQ)
    modulation = jnp.dot(time_code, mod_w, preferred_element_type=jnp.float32)
    shift_vec = modulation[:, :D]
    scale_vec = modulation[:, D:2 * D]
    gate_vec = modulation[:, 2 * D:]
    tile_tokens = all_tiles(latent.astype(jnp.bfloat16))
    chosen_ids = jnp.nonzero(cloudy, size=OWNERS)[0].astype(jnp.int32)
    chosen = tile_tokens[chosen_ids]

    def one_tile(single):
        return denoise_tiles(single[None], embed_w, pos_embed, shift_vec, scale_vec, gate_vec, wq, wk, wv, wo, q_gain, k_gain, out_w)[0]
    eps_chosen = lax.map(one_tile, chosen)
    eps_tiles = jnp.zeros((TILES, TT, PV), jnp.bfloat16).at[chosen_ids].set(eps_chosen)
    eps_latent = all_pixels(eps_tiles.astype(jnp.float32))
    grid = cloudy.reshape(N_TILE, TILES_DEV)
    cloud_pixels = jnp.repeat(jnp.repeat(grid, TPX, axis=0), TPX, axis=1) == 1
    raw_estimate = jnp.where(cloud_pixels[None], (latent - sin_now * eps_latent) / cos_now, observed)
    padded = jnp.pad(raw_estimate, ((0, 0), (1, 1), (1, 1)))
    blended = jnp.zeros_like(raw_estimate)
    for row_shift in range(3):
        for col_shift in range(3):
            window = padded[:, row_shift:row_shift + HL, col_shift:col_shift + WL]
            blended = blended + jnp.einsum('oc,chw->ohw', conv_w[3 * row_shift + col_shift], window, precision=lax.Precision.HIGHEST)
    row_pos = jnp.arange(HL) % TPX
    col_pos = jnp.arange(WL) % TPX
    seam_mask = ((row_pos == 0) | (row_pos == TPX - 1))[:, None] | ((col_pos == 0) | (col_pos == TPX - 1))[None, :]
    estimate = jnp.where(seam_mask[None], blended, raw_estimate)
    next_latent = cos_prev * estimate + sin_prev * noise
    return (estimate, next_latent)
```

```python
import math

import jax
import jax.numpy as jnp
from jax import lax
from jax.experimental import pallas as pl
from jax.experimental.pallas import tpu as pltpu
from jax.sharding import PartitionSpec as P

HD = 128
PATCH = 2
MAXOWN = 3
TSTEPS = 1000
STRIDE = 20


def padded_2(block, sides, width):
    for axis, dim in sides:
        count = lax.axis_size(axis)
        forward = [(i, i + 1) for i in range(count - 1)]
        backward = [(target, source) for source, target in forward]
        low = lax.ppermute(
            lax.slice_in_dim(block, block.shape[dim] - width, None, axis=dim), axis, forward
        )
        high = lax.ppermute(lax.slice_in_dim(block, 0, width, axis=dim), axis, backward)
        block = jnp.concatenate([low, block, high], axis=dim)
    return block


def plan(step):
    theta = (step / TSTEPS + 0.008) / 1.008 * (math.pi / 2)
    return (jnp.cos(theta), jnp.sin(theta))


def time_features(step, width):
    half = width // 2
    freqs = jnp.exp(-math.log(10000.0) * jnp.arange(half, dtype=jnp.float32) / half)
    angles = step * freqs
    code = jnp.concatenate([jnp.cos(angles), jnp.sin(angles)])[None, :]
    return jax.nn.silu(code).astype(jnp.bfloat16)


def band_tiles(band, tile_side):
    channels, band_rows, band_cols = band.shape
    tiles_here = band_cols // (tile_side * PATCH)
    shaped = band.reshape(channels, tile_side, PATCH, tiles_here, tile_side, PATCH)
    return jnp.transpose(shaped, (3, 2, 5, 0, 1, 4)).reshape(
        tiles_here, PATCH * PATCH * channels, tile_side * tile_side
    )


def band_pixels(tiled, tile_side, channels):
    tiles_here = tiled.shape[0]
    shaped = tiled.reshape(tiles_here, PATCH, PATCH, channels, tile_side, tile_side)
    return jnp.transpose(shaped, (3, 4, 1, 0, 5, 2)).reshape(
        channels, tile_side * PATCH, tiles_here * tile_side * PATCH
    )


def centered(values):
    values = values.astype(jnp.float32)
    return values - jnp.mean(values, axis=-1, keepdims=True)


def norm_rows(values):
    center = values - jnp.mean(values, axis=0, keepdims=True)
    spread = jnp.mean(center * center, axis=0, keepdims=True)
    return center, lax.rsqrt(spread + 1e-06)


def denoise_kernel(tok_ref, fold_ref, wo_ref, emb_ref, pos_ref, gate_ref, out_w_ref, qg_ref, kg_ref, eps_ref, mix_ref):
    tokens = tok_ref[0]
    token_count = tokens.shape[1]
    per = fold_ref.shape[2]
    group = HD // per
    heads = mix_ref.shape[0] // HD
    h0 = jnp.dot(emb_ref[...], tokens, preferred_element_type=jnp.float32) + pos_ref[...].astype(jnp.float32)
    _, rstd = norm_rows(h0)

    def project(kind, head):
        block = fold_ref[pl.ds(head * group, group), kind].reshape(HD, fold_ref.shape[3])
        base = block[:, :token_count].astype(jnp.float32)
        own = jnp.dot(block[:, token_count : token_count + tokens.shape[0]], tokens, preferred_element_type=jnp.float32)
        last = token_count + tokens.shape[0]
        return (own + base) * rstd + block[:, last : last + 1].astype(jnp.float32)

    def head_norm(proj, gain):
        spread = jnp.mean(proj * proj, axis=0, keepdims=True)
        return (proj * lax.rsqrt(spread + 1e-06) * gain).astype(jnp.bfloat16)

    for head in range(heads):
        query = head_norm(project(0, head), qg_ref[...])
        key = head_norm(project(1, head), kg_ref[...])
        value = project(2, head).astype(jnp.bfloat16)
        scores = lax.dot_general(key, query, (((0,), (0,)), ((), ())), preferred_element_type=jnp.float32) * HD ** (-0.5)
        expo = jnp.exp(scores - jnp.max(scores, axis=0, keepdims=True))
        probs = (expo * (1.0 / jnp.sum(expo, axis=0, keepdims=True))).astype(jnp.bfloat16)
        mixed = jnp.dot(value, probs, preferred_element_type=jnp.float32)
        mix_ref[head * HD : (head + 1) * HD, :] = mixed.astype(jnp.bfloat16)
    attn = jnp.dot(wo_ref[...], mix_ref[...], preferred_element_type=jnp.float32)
    center, rstd1 = norm_rows(h0 + gate_ref[...] * attn)
    final = (center * rstd1).astype(jnp.bfloat16)
    eps_ref[0] = jnp.dot(out_w_ref[...], final, preferred_element_type=jnp.float32).astype(jnp.bfloat16)


def denoise(chosen, embed_w, pos_embed, shift_vec, scale_vec, gate_vec, wq, wk, wv, wo, q_gain, k_gain, out_w):
    parts = lax.axis_size("tile")
    tiles, token_values, token_count = chosen.shape
    width = embed_w.shape[1]
    inner = wq.shape[1]
    per = inner // parts
    rows = wq.shape[0]
    stacked = jnp.stack([wq, wk, wv], axis=1).reshape(rows, 3, parts, per)
    chunks = jnp.transpose(stacked, (2, 0, 1, 3)).reshape(parts, rows, 3 * per)
    mine = lax.all_to_all(chunks, "tile", 0, 0, tiled=True).reshape(width, 3 * per)
    wo_t = lax.all_gather(wo.T, "tile", axis=0, tiled=True)
    folded = jnp.concatenate([centered(pos_embed), centered(embed_w)], axis=0) * (1.0 + scale_vec)
    pad = -(token_count + token_values + 1) % HD
    left = jnp.concatenate([folded, shift_vec, jnp.zeros((pad, width), jnp.float32)], axis=0).astype(jnp.bfloat16)
    fold = lax.dot_general(mine, left, (((0,), (1,)), ((), ())), preferred_element_type=jnp.float32)
    fold = fold.astype(jnp.bfloat16).reshape(1, 3, per, left.shape[0])
    fold_all = lax.all_gather(fold, "tile", axis=0, tiled=True)
    args = (chosen, fold_all, wo_t, embed_w.T, pos_embed.T, gate_vec.reshape(-1, 1), out_w.T, q_gain.reshape(-1, 1), k_gain.reshape(-1, 1))
    whole = [pl.BlockSpec(memory_space=pltpu.VMEM)] * (len(args) - 1)
    block = pl.BlockSpec((1, token_values, token_count), lambda i: (i, 0, 0))
    return pl.pallas_call(
        denoise_kernel,
        grid=(tiles,),
        out_shape=jax.ShapeDtypeStruct(chosen.shape, jnp.bfloat16),
        in_specs=[block] + whole,
        out_specs=block,
        scratch_shapes=[pltpu.VMEM((inner, token_count), jnp.bfloat16)],
        compiler_params=pltpu.CompilerParams(vmem_limit_bytes=48 * 1024 * 1024),
    )(*args)


def on_device(
    latent,
    observed,
    noise,
    cloudy,
    timestep,
    pos_embed,
    embed_w,
    mod_w,
    wq,
    wk,
    wv,
    wo,
    q_gain,
    k_gain,
    out_w,
    conv_w,
):
    channels, band_rows, band_cols = latent.shape
    tile_side = band_rows // PATCH
    tiles_here = band_cols // band_rows
    width = embed_w.shape[1]
    step_now = timestep[0].astype(jnp.float32)
    cos_now, sin_now = plan(step_now)
    cos_prev, sin_prev = plan(step_now - STRIDE)
    time_code = time_features(step_now, mod_w.shape[0])
    local_mod = jnp.dot(time_code, mod_w, preferred_element_type=jnp.float32)
    modulation = lax.all_gather(local_mod, "tile", axis=1, tiled=True)
    shift_vec = modulation[:, :width]
    scale_vec = modulation[:, width : 2 * width]
    gate_vec = modulation[:, 2 * width :]
    tile_tokens = band_tiles(latent.astype(jnp.bfloat16), tile_side)
    order_in = jnp.cumsum(cloudy) - cloudy
    weights_all = (
        embed_w,
        pos_embed,
        shift_vec,
        scale_vec,
        gate_vec,
        wq,
        wk,
        wv,
        wo,
        q_gain,
        k_gain,
        out_w,
    )
    slot_ids = jnp.arange(MAXOWN, dtype=jnp.int32)
    slot_hit = (cloudy[None, :] == 1) & (order_in[None, :] == slot_ids[:, None])
    picked = jnp.sum(
        jnp.where(slot_hit, jnp.arange(tiles_here, dtype=jnp.int32)[None, :], 0), axis=1
    )
    chosen = jnp.take(tile_tokens, picked, axis=0)
    eps_chosen = denoise(chosen, *weights_all)
    eps_back = jnp.take(eps_chosen, jnp.minimum(order_in, MAXOWN - 1), axis=0)
    eps_tiles = jnp.where(cloudy[:, None, None] == 1, eps_back, jnp.zeros_like(eps_back))
    eps_latent = band_pixels(eps_tiles.astype(jnp.float32), tile_side, channels)
    cloud_cols = jnp.repeat(cloudy, band_rows) == 1
    raw_estimate = jnp.where(
        cloud_cols[None, None, :], (latent - sin_now * eps_latent) / cos_now, observed
    )
    padded = padded_2(raw_estimate, (("tile", 1),), 1)
    padded = jnp.pad(padded, ((0, 0), (0, 0), (1, 1)))
    blended = jnp.zeros_like(raw_estimate)
    for row_shift in range(3):
        for col_shift in range(3):
            window = padded[:, row_shift : row_shift + band_rows, col_shift : col_shift + band_cols]
            blended = blended + jnp.einsum(
                "oc,chw->ohw",
                conv_w[3 * row_shift + col_shift],
                window,
                precision=lax.Precision.HIGHEST,
            )
    row_pos = jnp.arange(band_rows) % band_rows
    col_pos = jnp.arange(band_cols) % band_rows
    seam_mask = ((row_pos == 0) | (row_pos == band_rows - 1))[:, None] | (
        (col_pos == 0) | (col_pos == band_rows - 1)
    )[None, :]
    estimate = jnp.where(seam_mask[None], blended, raw_estimate)
    next_latent = cos_prev * estimate + sin_prev * noise
    return (estimate, next_latent)


def solution(mesh):
    placed = (
        P(None, ("grp", "tile"), None),
        P(None, ("grp", "tile"), None),
        P(None, ("grp", "tile"), None),
        P(("grp", "tile")),
        P("grp"),
        P(),
        P(),
        P(None, "tile"),
        P("tile", None),
        P("tile", None),
        P("tile", None),
        P(None, "tile"),
        P(),
        P(),
        P(),
        P(),
    )
    return jax.shard_map(
        on_device,
        mesh=mesh,
        in_specs=placed,
        out_specs=(P(None, ("grp", "tile"), None), P(None, ("grp", "tile"), None)),
        check_vma=False,
    )
```

```python
import functools
import math

import jax
import jax.numpy as jnp
from jax import lax
from jax.experimental import pallas as pl
from jax.experimental.pallas import tpu as pltpu
from jax.sharding import PartitionSpec as P

HD = 128
PATCH = 2
MAXOWN = 3
TSTEPS = 1000
STRIDE = 20


def padded_2(block, sides, width):
    for axis, dim in sides:
        count = lax.axis_size(axis)
        forward = [(i, i + 1) for i in range(count - 1)]
        backward = [(target, source) for source, target in forward]
        low = lax.ppermute(
            lax.slice_in_dim(block, block.shape[dim] - width, None, axis=dim), axis, forward
        )
        high = lax.ppermute(lax.slice_in_dim(block, 0, width, axis=dim), axis, backward)
        block = jnp.concatenate([low, block, high], axis=dim)
    return block


def plan(step):
    theta = (step / TSTEPS + 0.008) / 1.008 * (math.pi / 2)
    return (jnp.cos(theta), jnp.sin(theta))


def time_features(step, width):
    half = width // 2
    freqs = jnp.exp(-math.log(10000.0) * jnp.arange(half, dtype=jnp.float32) / half)
    angles = step * freqs
    code = jnp.concatenate([jnp.cos(angles), jnp.sin(angles)])[None, :]
    return jax.nn.silu(code).astype(jnp.bfloat16)


def band_tiles(band, tile_side):
    channels, band_rows, band_cols = band.shape
    tiles_here = band_cols // (tile_side * PATCH)
    shaped = band.reshape(channels, tile_side, PATCH, tiles_here, tile_side, PATCH)
    return jnp.transpose(shaped, (3, 2, 5, 0, 1, 4)).reshape(
        tiles_here, PATCH * PATCH * channels, tile_side * tile_side
    )


def band_pixels(tiled, tile_side, channels):
    tiles_here = tiled.shape[0]
    shaped = tiled.reshape(tiles_here, PATCH, PATCH, channels, tile_side, tile_side)
    return jnp.transpose(shaped, (3, 4, 1, 0, 5, 2)).reshape(
        channels, tile_side * PATCH, tiles_here * tile_side * PATCH
    )


def centered(values):
    values = values.astype(jnp.float32)
    return values - jnp.mean(values, axis=-1, keepdims=True)


LO = 4


def send(src, dst, sems, slot, target):
    copy = pltpu.make_async_remote_copy(
        src_ref=src,
        dst_ref=dst,
        send_sem=sems[0].at[slot],
        recv_sem=sems[1].at[slot],
        device_id={"tile": target},
        device_id_type=pl.DeviceIdType.MESH,
    )
    copy.start()
    return copy


def greet(targets):
    barrier = pltpu.get_barrier_semaphore()
    for target in targets:
        pl.semaphore_signal(barrier, inc=1, device_id={"tile": target}, device_id_type=pl.DeviceIdType.MESH)
    pl.semaphore_wait(barrier, len(targets))


def pair(count):
    return [pltpu.SemaphoreType.DMA((count,)), pltpu.SemaphoreType.DMA((count,))]


def spread_kernel(parts, mod_ref, chunk_ref, wo_ref, mods_ref, mine_ref, line_ref, ms, mr, cs, cr, ws, wr):
    me = lax.axis_index("tile")
    level, lane = me // LO, lax.rem(me, LO)
    levels = parts // LO
    others = [lax.rem(me + k, parts) for k in range(1, parts)]
    greet(others)
    copies = []
    for k, target in enumerate(others):
        copies.append(send(mod_ref, mods_ref.at[me], (ms, mr), k, target))
    for k, target in enumerate(others):
        copies.append(send(chunk_ref.at[target], mine_ref.at[me], (cs, cr), k, target))
    for k in range(1, levels):
        target = lax.rem(level + k, levels) * LO + lane
        copies.append(send(wo_ref, line_ref.at[level], (ws, wr), k - 1, target))
    mods_ref[me] = mod_ref[...]
    mine_ref[me] = chunk_ref[me]
    line_ref[level] = wo_ref[...]
    for copy in copies:
        copy.wait_recv()
    for copy in copies:
        copy.wait_send()


def norm_rows(values):
    center = values - jnp.mean(values, axis=0, keepdims=True)
    spread = jnp.mean(center * center, axis=0, keepdims=True)
    return center, lax.rsqrt(spread + 1e-06)


def denoise_kernel(
    parts,
    tok_ref,
    fold_ref,
    line_ref,
    emb_ref,
    pos_ref,
    gate_ref,
    out_w_ref,
    qg_ref,
    kg_ref,
    eps_ref,
    all_ref,
    wo_ref,
    h0_ref,
    mix_ref,
    fzs,
    fzr,
    fys,
    fyr,
    fcs,
    fcr,
    wys,
    wyr,
    wcs,
    wcr,
):
    me = lax.axis_index("tile")
    level, lane = me // LO, lax.rem(me, LO)
    levels = parts // LO
    side = lax.rem(lane + 2, LO)
    twin = lane + 1 - 2 * lax.rem(lane, 2)
    line = [lax.rem(level + k, levels) * LO + lane for k in range(1, levels)]
    beside, mate = level * LO + side, level * LO + twin
    greet(line + [beside, mate])

    sends = []
    z_copies = [send(fold_ref, all_ref.at[me], (fzs, fzr), k, target) for k, target in enumerate(line)]
    all_ref[me] = fold_ref[...]
    y_copies = [send(fold_ref, all_ref.at[me], (fys, fyr), 0, beside)]
    c_copies = [send(fold_ref, all_ref.at[me], (fcs, fcr), 0, mate)]
    wy_copies, wc_copies = [], []
    for k in range(levels):
        at = lax.rem(level + levels - k, levels)
        slot = at * LO + lane
        wy_copies.append(send(line_ref.at[at], wo_ref.at[slot], (wys, wyr), k, beside))
        wc_copies.append(send(line_ref.at[at], wo_ref.at[slot], (wcs, wcr), k, mate))
        wo_ref[slot] = line_ref[at]

    tiles, token_values, token_count = tok_ref.shape
    per = fold_ref.shape[1]
    group = HD // per
    heads = mix_ref.shape[1] // HD
    rstds = []
    for tile in range(tiles):
        h0 = jnp.dot(emb_ref[...], tok_ref[tile], preferred_element_type=jnp.float32) + pos_ref[...].astype(jnp.float32)
        h0_ref[tile] = h0
        rstds.append(norm_rows(h0)[1])

    for k, copy in enumerate(z_copies):
        copy.wait_recv()
        slot = lax.rem(level + levels - k - 1, levels) * LO + lane
        y_copies.append(send(all_ref.at[slot], all_ref.at[slot], (fys, fyr), k + 1, beside))
        c_copies.append(send(all_ref.at[slot], all_ref.at[slot], (fcs, fcr), k + 1, mate))
    for k in range(levels):
        y_copies[k].wait_recv()
        slot = lax.rem(level + levels - k, levels) * LO + side
        c_copies.append(send(all_ref.at[slot], all_ref.at[slot], (fcs, fcr), levels + k, mate))
    for copy in c_copies:
        copy.wait_recv()
    for k in range(levels):
        wy_copies[k].wait_recv()
        slot = lax.rem(level + levels - k, levels) * LO + side
        wc_copies.append(send(wo_ref.at[slot], wo_ref.at[slot], (wcs, wcr), levels + k, mate))

    def head_norm(proj, gain):
        spread = jnp.mean(proj * proj, axis=0, keepdims=True)
        return (proj * lax.rsqrt(spread + 1e-06) * gain).astype(jnp.bfloat16)

    last = token_count + token_values

    @pl.loop(0, heads)
    def _(head):
        blocks = [all_ref[pl.ds(head * group, group), kind].reshape(HD, fold_ref.shape[2]) for kind in range(3)]
        for tile in range(tiles):
            parts3 = []
            for block in blocks:
                own = jnp.dot(block[:, token_count:last], tok_ref[tile], preferred_element_type=jnp.float32)
                proj = (own + block[:, :token_count].astype(jnp.float32)) * rstds[tile]
                parts3.append(proj + block[:, last : last + 1].astype(jnp.float32))
            query = head_norm(parts3[0], qg_ref[...])
            key = head_norm(parts3[1], kg_ref[...])
            value = parts3[2].astype(jnp.bfloat16)
            scores = lax.dot_general(key, query, (((0,), (0,)), ((), ())), preferred_element_type=jnp.float32) * HD ** (-0.5)
            expo = jnp.exp(scores - jnp.max(scores, axis=0, keepdims=True))
            probs = (expo * (1.0 / jnp.sum(expo, axis=0, keepdims=True))).astype(jnp.bfloat16)
            mixed = jnp.dot(value, probs, preferred_element_type=jnp.float32)
            mix_ref[tile, pl.ds(pl.multiple_of(head * HD, HD), HD), :] = mixed.astype(jnp.bfloat16)

    for copy in wc_copies:
        copy.wait_recv()
    wo_t = wo_ref[...].reshape(-1, wo_ref.shape[2])
    for tile in range(tiles):
        attn = jnp.dot(wo_t, mix_ref[tile], preferred_element_type=jnp.float32)
        center, rstd1 = norm_rows(h0_ref[tile] + gate_ref[...] * attn)
        final = (center * rstd1).astype(jnp.bfloat16)
        eps_ref[tile] = jnp.dot(out_w_ref[...], final, preferred_element_type=jnp.float32).astype(jnp.bfloat16)
    for copy in z_copies + y_copies + c_copies + wy_copies + wc_copies:
        copy.wait_send()


def denoise(chosen, embed_w, pos_embed, local_mod, wq, wk, wv, wo, q_gain, k_gain, out_w):
    parts = lax.axis_size("tile")
    levels = parts // LO
    tiles, token_values, token_count = chosen.shape
    width = embed_w.shape[1]
    inner = wq.shape[1]
    per = inner // parts
    rows = wq.shape[0]
    stacked = jnp.stack([wq, wk, wv], axis=1).reshape(rows, 3, parts, per)
    chunks = jnp.transpose(stacked, (2, 0, 1, 3)).reshape(parts, rows, 3 * per)
    wo_t = wo.T
    mod_rows = jnp.broadcast_to(local_mod, (8, local_mod.shape[1]))
    in_vmem = pl.BlockSpec(memory_space=pltpu.VMEM)
    mods, mine, line = pl.pallas_call(
        functools.partial(spread_kernel, parts),
        out_shape=(
            jax.ShapeDtypeStruct((parts,) + mod_rows.shape, jnp.float32),
            jax.ShapeDtypeStruct(chunks.shape, jnp.bfloat16),
            jax.ShapeDtypeStruct((levels,) + wo_t.shape, jnp.bfloat16),
        ),
        in_specs=[in_vmem] * 3,
        out_specs=(in_vmem,) * 3,
        scratch_shapes=pair(parts) + pair(parts) + pair(levels),
        compiler_params=pltpu.CompilerParams(collective_id=0, has_side_effects=True, vmem_limit_bytes=32 * 1024 * 1024),
    )(mod_rows, chunks, wo_t)
    mine = mine.reshape(width, 3 * per)
    modulation = mods[:, 0].reshape(1, -1)
    shift_vec = modulation[:, :width]
    scale_vec = modulation[:, width : 2 * width]
    gate_vec = modulation[:, 2 * width :]
    folded = jnp.concatenate([centered(pos_embed), centered(embed_w)], axis=0) * (1.0 + scale_vec)
    pad = -(token_count + token_values + 1) % HD
    left = jnp.concatenate([folded, shift_vec, jnp.zeros((pad, width), jnp.float32)], axis=0).astype(jnp.bfloat16)
    fold = lax.dot_general(mine, left, (((0,), (1,)), ((), ())), preferred_element_type=jnp.float32)
    fold = fold.astype(jnp.bfloat16).reshape(3, per, left.shape[0])
    args = (chosen, fold, line, embed_w.T, pos_embed.T, gate_vec.reshape(-1, 1), out_w.T, q_gain.reshape(-1, 1), k_gain.reshape(-1, 1))
    return pl.pallas_call(
        functools.partial(denoise_kernel, parts),
        out_shape=jax.ShapeDtypeStruct(chosen.shape, jnp.bfloat16),
        in_specs=[in_vmem] * len(args),
        out_specs=in_vmem,
        scratch_shapes=[
            pltpu.VMEM((parts,) + fold.shape, jnp.bfloat16),
            pltpu.VMEM((parts,) + wo_t.shape, jnp.bfloat16),
            pltpu.VMEM((tiles, width, token_count), jnp.float32),
            pltpu.VMEM((tiles, inner, token_count), jnp.bfloat16),
        ]
        + pair(levels)
        + pair(levels)
        + pair(2 * levels)
        + pair(levels)
        + pair(2 * levels),
        compiler_params=pltpu.CompilerParams(collective_id=1, has_side_effects=True, vmem_limit_bytes=56 * 1024 * 1024),
    )(*args)


def on_device(
    latent,
    observed,
    noise,
    cloudy,
    timestep,
    pos_embed,
    embed_w,
    mod_w,
    wq,
    wk,
    wv,
    wo,
    q_gain,
    k_gain,
    out_w,
    conv_w,
):
    channels, band_rows, band_cols = latent.shape
    tile_side = band_rows // PATCH
    tiles_here = band_cols // band_rows
    step_now = timestep[0].astype(jnp.float32)
    cos_now, sin_now = plan(step_now)
    cos_prev, sin_prev = plan(step_now - STRIDE)
    time_code = time_features(step_now, mod_w.shape[0])
    local_mod = jnp.dot(time_code, mod_w, preferred_element_type=jnp.float32)
    tile_tokens = band_tiles(latent.astype(jnp.bfloat16), tile_side)
    order_in = jnp.cumsum(cloudy) - cloudy
    weights_all = (
        embed_w,
        pos_embed,
        local_mod,
        wq,
        wk,
        wv,
        wo,
        q_gain,
        k_gain,
        out_w,
    )
    slot_ids = jnp.arange(MAXOWN, dtype=jnp.int32)
    slot_hit = (cloudy[None, :] == 1) & (order_in[None, :] == slot_ids[:, None])
    picked = jnp.sum(
        jnp.where(slot_hit, jnp.arange(tiles_here, dtype=jnp.int32)[None, :], 0), axis=1
    )
    chosen = jnp.take(tile_tokens, picked, axis=0)
    eps_chosen = denoise(chosen, *weights_all)
    eps_back = jnp.take(eps_chosen, jnp.minimum(order_in, MAXOWN - 1), axis=0)
    eps_tiles = jnp.where(cloudy[:, None, None] == 1, eps_back, jnp.zeros_like(eps_back))
    eps_latent = band_pixels(eps_tiles.astype(jnp.float32), tile_side, channels)
    cloud_cols = jnp.repeat(cloudy, band_rows) == 1
    raw_estimate = jnp.where(
        cloud_cols[None, None, :], (latent - sin_now * eps_latent) / cos_now, observed
    )
    padded = padded_2(raw_estimate, (("tile", 1),), 1)
    padded = jnp.pad(padded, ((0, 0), (0, 0), (1, 1)))
    blended = jnp.zeros_like(raw_estimate)
    for row_shift in range(3):
        for col_shift in range(3):
            window = padded[:, row_shift : row_shift + band_rows, col_shift : col_shift + band_cols]
            blended = blended + jnp.einsum(
                "oc,chw->ohw",
                conv_w[3 * row_shift + col_shift],
                window,
                precision=lax.Precision.HIGHEST,
            )
    row_pos = jnp.arange(band_rows) % band_rows
    col_pos = jnp.arange(band_cols) % band_rows
    seam_mask = ((row_pos == 0) | (row_pos == band_rows - 1))[:, None] | (
        (col_pos == 0) | (col_pos == band_rows - 1)
    )[None, :]
    estimate = jnp.where(seam_mask[None], blended, raw_estimate)
    next_latent = cos_prev * estimate + sin_prev * noise
    return (estimate, next_latent)


def solution(mesh):
    placed = (
        P(None, ("grp", "tile"), None),
        P(None, ("grp", "tile"), None),
        P(None, ("grp", "tile"), None),
        P(("grp", "tile")),
        P("grp"),
        P(),
        P(),
        P(None, "tile"),
        P("tile", None),
        P("tile", None),
        P("tile", None),
        P(None, "tile"),
        P(),
        P(),
        P(),
        P(),
    )
    return jax.shard_map(
        on_device,
        mesh=mesh,
        in_specs=placed,
        out_specs=(P(None, ("grp", "tile"), None), P(None, ("grp", "tile"), None)),
        check_vma=False,
    )
```

```python
import functools
import math

import jax
import jax.numpy as jnp
from jax import lax
from jax.experimental import pallas as pl
from jax.experimental.pallas import tpu as pltpu
from jax.sharding import PartitionSpec as P

HD = 128
PATCH = 2
MAXOWN = 3
TSTEPS = 1000
STRIDE = 20


def padded_2(block, sides, width):
    for axis, dim in sides:
        count = lax.axis_size(axis)
        forward = [(i, i + 1) for i in range(count - 1)]
        backward = [(target, source) for source, target in forward]
        low = lax.ppermute(
            lax.slice_in_dim(block, block.shape[dim] - width, None, axis=dim), axis, forward
        )
        high = lax.ppermute(lax.slice_in_dim(block, 0, width, axis=dim), axis, backward)
        block = jnp.concatenate([low, block, high], axis=dim)
    return block


def plan(step):
    theta = (step / TSTEPS + 0.008) / 1.008 * (math.pi / 2)
    return (jnp.cos(theta), jnp.sin(theta))


def time_features(step, width):
    half = width // 2
    freqs = jnp.exp(-math.log(10000.0) * jnp.arange(half, dtype=jnp.float32) / half)
    angles = step * freqs
    code = jnp.concatenate([jnp.cos(angles), jnp.sin(angles)])[None, :]
    return jax.nn.silu(code).astype(jnp.bfloat16)


def band_tiles(band, tile_side):
    channels, band_rows, band_cols = band.shape
    tiles_here = band_cols // (tile_side * PATCH)
    shaped = band.reshape(channels, tile_side, PATCH, tiles_here, tile_side, PATCH)
    return jnp.transpose(shaped, (3, 2, 5, 0, 1, 4)).reshape(
        tiles_here, PATCH * PATCH * channels, tile_side * tile_side
    )


def band_pixels(tiled, tile_side, channels):
    tiles_here = tiled.shape[0]
    shaped = tiled.reshape(tiles_here, PATCH, PATCH, channels, tile_side, tile_side)
    return jnp.transpose(shaped, (3, 4, 1, 0, 5, 2)).reshape(
        channels, tile_side * PATCH, tiles_here * tile_side * PATCH
    )


def centered(values):
    values = values.astype(jnp.float32)
    return values - jnp.mean(values, axis=-1, keepdims=True)


LO = 4


def send(src, dst, sems, slot, target):
    copy = pltpu.make_async_remote_copy(
        src_ref=src,
        dst_ref=dst,
        send_sem=sems[0].at[slot],
        recv_sem=sems[1].at[slot],
        device_id=target,
        device_id_type=pl.DeviceIdType.MESH,
    )
    copy.start()
    return copy


def pair(count):
    return [pltpu.SemaphoreType.DMA((count,)), pltpu.SemaphoreType.DMA((count,))]


def norm_rows(values):
    center = values - jnp.mean(values, axis=0, keepdims=True)
    spread = jnp.mean(center * center, axis=0, keepdims=True)
    return center, lax.rsqrt(spread + 1e-06)


def column(row):
    return jnp.broadcast_to(row, (8, row.shape[1])).T[:, 0:1]


def denoise_kernel(
    parts,
    tok_ref,
    mod_ref,
    wq_ref,
    wk_ref,
    wv_ref,
    wo_in_ref,
    emb_ref,
    pos_ref,
    out_w_ref,
    qg_ref,
    kg_ref,
    eps_ref,
    chunk_ref,
    mods_ref,
    mine_ref,
    left_ref,
    all_ref,
    wo_ref,
    h0_ref,
    mix_ref,
    ms,
    mr,
    cs,
    cr,
    fzs,
    fzr,
    fys,
    fyr,
    fcs,
    fcr,
    wzs,
    wzr,
    wys,
    wyr,
    wxs,
    wxr,
    wcs,
    wcr,
):
    me = lax.axis_index("tile")
    grp = lax.axis_index("grp")
    half = lax.rem(grp, 2)
    rest = 1 - half
    across = grp + 1 - 2 * half
    level, lane = me // LO, lax.rem(me, LO)
    levels = parts // LO
    side = lax.rem(lane + 2, LO)
    twin = lane + 1 - 2 * lax.rem(lane, 2)
    others = [lax.rem(me + k, parts) for k in range(1, parts)]
    line = [lax.rem(level + k, levels) * LO + lane for k in range(1, levels)]
    beside, mate = level * LO + side, level * LO + twin
    lane_slots = [lax.rem(level + levels - k, levels) * LO + lane for k in range(levels)]
    side_slots = [lax.rem(level + levels - k, levels) * LO + side for k in range(levels)]

    barrier = pltpu.get_barrier_semaphore()
    for target in others:
        pl.semaphore_signal(barrier, inc=1, device_id={"tile": target}, device_id_type=pl.DeviceIdType.MESH)
    pl.semaphore_signal(barrier, inc=1, device_id={"grp": across}, device_id_type=pl.DeviceIdType.MESH)

    per = wq_ref.shape[1] // parts
    for part in range(parts):
        pieces = [ref[:, part * per : (part + 1) * per] for ref in (wq_ref, wk_ref, wv_ref)]
        chunk_ref[part] = jnp.concatenate(pieces, axis=1)
    pl.semaphore_wait(barrier, parts)

    mod_copies = [send(mod_ref, mods_ref.at[me], (ms, mr), k, {"tile": t}) for k, t in enumerate(others)]
    chunk_copies = [send(chunk_ref.at[t], mine_ref.at[me], (cs, cr), k, {"tile": t}) for k, t in enumerate(others)]
    mods_ref[me] = mod_ref[...]
    mine_ref[me] = chunk_ref[me]
    wo_ref[me] = wo_in_ref[...]

    tiles, token_values, token_count = tok_ref.shape
    width = emb_ref.shape[1]
    pos = pos_ref[...].astype(jnp.float32)
    pos_t = pos.T
    rstds = []
    for tile in range(tiles):
        own = lax.dot_general(emb_ref[...], tok_ref[tile], (((0,), (0,)), ((), ())), preferred_element_type=jnp.float32)
        h0 = own + pos_t
        h0_ref[tile] = h0
        rstds.append(norm_rows(h0)[1])
    query_gain, key_gain = column(qg_ref[...]), column(kg_ref[...])
    for copy in mod_copies:
        copy.wait_recv()
    modulation = jnp.concatenate([mods_ref[part] for part in range(parts)], axis=1)
    scale = 1.0 + modulation[0:1, width : 2 * width]
    gate = modulation[:, 2 * width :].T[:, 0:1]
    last = token_count + token_values
    left_ref[:token_count] = (centered(pos) * scale).astype(jnp.bfloat16)
    left_ref[token_count:last] = (centered(emb_ref[...]) * scale).astype(jnp.bfloat16)
    left_ref[last:] = jnp.broadcast_to(modulation[0:1, :width], (left_ref.shape[0] - last, width)).astype(jnp.bfloat16)
    for copy in chunk_copies:
        copy.wait_recv()

    mine = mine_ref[...].reshape(width, 3 * per)
    fold = lax.dot_general(mine, left_ref[...], (((0,), (1,)), ((), ())), preferred_element_type=jnp.float32)
    all_ref[me] = fold.astype(jnp.bfloat16).reshape(3, per, left_ref.shape[0])

    z_copies = [send(all_ref.at[me], all_ref.at[me], (fzs, fzr), k, {"tile": t}) for k, t in enumerate(line)]
    y_copies = [send(all_ref.at[me], all_ref.at[me], (fys, fyr), 0, {"tile": beside})]
    c_copies = [send(all_ref.at[me], all_ref.at[me], (fcs, fcr), 0, {"tile": mate})]
    wz_copies = [
        send(wo_ref.at[me, half], wo_ref.at[me, half], (wzs, wzr), k, {"tile": t}) for k, t in enumerate(line)
    ]
    for k, copy in enumerate(z_copies):
        copy.wait_recv()
        block = all_ref.at[lane_slots[k + 1]]
        y_copies.append(send(block, block, (fys, fyr), k + 1, {"tile": beside}))
        c_copies.append(send(block, block, (fcs, fcr), k + 1, {"tile": mate}))
    wy_copies, wx_copies, wc_copies = [], [], []

    def pass_wo(copies, sems, slot, which, target):
        block = wo_ref.at[slot, which]
        copies.append(send(block, block, sems, len(copies), target))

    pass_wo(wy_copies, (wys, wyr), me, half, {"tile": beside})
    pass_wo(wc_copies, (wcs, wcr), me, half, {"tile": mate})
    pass_wo(wc_copies, (wcs, wcr), me, rest, {"tile": mate})
    for k in range(1, levels):
        wz_copies[k - 1].wait_recv()
        pass_wo(wy_copies, (wys, wyr), lane_slots[k], half, {"tile": beside})
        pass_wo(wx_copies, (wxs, wxr), lane_slots[k], half, {"grp": across})
        pass_wo(wc_copies, (wcs, wcr), lane_slots[k], half, {"tile": mate})
    for k in range(levels):
        y_copies[k].wait_recv()
        block = all_ref.at[side_slots[k]]
        c_copies.append(send(block, block, (fcs, fcr), levels + k, {"tile": mate}))
    for copy in c_copies:
        copy.wait_recv()

    def head_norm(proj, gain):
        spread = jnp.mean(proj * proj, axis=0, keepdims=True)
        return (proj * lax.rsqrt(spread + 1e-06) * gain).astype(jnp.bfloat16)

    group = HD // per
    heads = mix_ref.shape[1] // HD

    def attend(head):
        blocks = [all_ref[pl.ds(head * group, group), kind].reshape(HD, all_ref.shape[3]) for kind in range(3)]
        for tile in range(tiles):
            projs = []
            for block in blocks:
                own = jnp.dot(block[:, token_count:last], tok_ref[tile], preferred_element_type=jnp.float32)
                proj = (own + block[:, :token_count].astype(jnp.float32)) * rstds[tile]
                projs.append(proj + block[:, last : last + 1].astype(jnp.float32))
            query = head_norm(projs[0], query_gain)
            key = head_norm(projs[1], key_gain)
            value = projs[2].astype(jnp.bfloat16)
            scores = lax.dot_general(key, query, (((0,), (0,)), ((), ())), preferred_element_type=jnp.float32) * HD ** (-0.5)
            expo = jnp.exp(scores - jnp.max(scores, axis=0, keepdims=True))
            probs = (expo * (1.0 / jnp.sum(expo, axis=0, keepdims=True))).astype(jnp.bfloat16)
            mixed = jnp.dot(value, probs, preferred_element_type=jnp.float32)
            mix_ref[tile, pl.ds(pl.multiple_of(head * HD, HD), HD), :] = mixed.astype(jnp.bfloat16)

    pl.loop(0, heads // 4)(attend)
    for k in range(levels):
        wy_copies[k].wait_recv()
        pass_wo(wx_copies, (wxs, wxr), side_slots[k], half, {"grp": across})
        pass_wo(wc_copies, (wcs, wcr), side_slots[k], half, {"tile": mate})
    pl.loop(heads // 4, heads - heads // 4)(attend)
    for k, slot in enumerate(lane_slots[1:] + side_slots):
        wx_copies[k].wait_recv()
        pass_wo(wc_copies, (wcs, wcr), slot, rest, {"tile": mate})
    pl.loop(heads - heads // 4, heads)(attend)
    for copy in wc_copies:
        copy.wait_recv()

    wo_t = wo_ref[...].reshape(width, wo_ref.shape[3])
    for tile in range(tiles):
        attn = jnp.dot(wo_t, mix_ref[tile], preferred_element_type=jnp.float32)
        center, rstd1 = norm_rows(h0_ref[tile] + gate * attn)
        final = (center * rstd1).astype(jnp.bfloat16)
        eps = lax.dot_general(out_w_ref[...], final, (((0,), (0,)), ((), ())), preferred_element_type=jnp.float32)
        eps_ref[tile] = eps.astype(jnp.bfloat16)
    for copies in (mod_copies, chunk_copies, z_copies, y_copies, c_copies, wz_copies, wy_copies, wx_copies, wc_copies):
        for copy in copies:
            copy.wait_send()


def denoise(chosen, embed_w, pos_embed, local_mod, wq, wk, wv, wo, q_gain, k_gain, out_w):
    parts = lax.axis_size("tile")
    levels = parts // LO
    tiles, token_values, token_count = chosen.shape
    width = embed_w.shape[1]
    rows, inner = wq.shape
    per = inner // parts
    wo_t = wo.T.reshape(2, -1, inner)
    mod_rows = jnp.broadcast_to(local_mod, (8, local_mod.shape[1]))
    depth = token_count + token_values + HD
    args = (chosen, mod_rows, wq, wk, wv, wo_t, embed_w, pos_embed, out_w, q_gain.reshape(1, -1), k_gain.reshape(1, -1))
    in_vmem = pl.BlockSpec(memory_space=pltpu.VMEM)
    bf16 = jnp.bfloat16
    return pl.pallas_call(
        functools.partial(denoise_kernel, parts),
        out_shape=jax.ShapeDtypeStruct(chosen.shape, bf16),
        in_specs=[in_vmem] * len(args),
        out_specs=in_vmem,
        scratch_shapes=[
            pltpu.VMEM((parts, rows, 3 * per), bf16),
            pltpu.VMEM((parts,) + mod_rows.shape, jnp.float32),
            pltpu.VMEM((parts, rows, 3 * per), bf16),
            pltpu.VMEM((depth, width), bf16),
            pltpu.VMEM((parts, 3, per, depth), bf16),
            pltpu.VMEM((parts,) + wo_t.shape, bf16),
            pltpu.VMEM((tiles, width, token_count), jnp.float32),
            pltpu.VMEM((tiles, inner, token_count), bf16),
        ]
        + pair(parts)
        + pair(parts)
        + pair(levels)
        + pair(levels)
        + pair(2 * levels)
        + pair(levels)
        + pair(levels)
        + pair(2 * levels)
        + pair(4 * levels),
        compiler_params=pltpu.CompilerParams(collective_id=0, has_side_effects=True, vmem_limit_bytes=60 * 1024 * 1024),
    )(*args)


def on_device(
    latent,
    observed,
    noise,
    cloudy,
    timestep,
    pos_embed,
    embed_w,
    mod_w,
    wq,
    wk,
    wv,
    wo,
    q_gain,
    k_gain,
    out_w,
    conv_w,
):
    channels, band_rows, band_cols = latent.shape
    tile_side = band_rows // PATCH
    tiles_here = band_cols // band_rows
    step_now = timestep[0].astype(jnp.float32)
    cos_now, sin_now = plan(step_now)
    cos_prev, sin_prev = plan(step_now - STRIDE)
    time_code = time_features(step_now, mod_w.shape[0])
    local_mod = jnp.dot(time_code, mod_w, preferred_element_type=jnp.float32)
    tile_tokens = band_tiles(latent.astype(jnp.bfloat16), tile_side)
    order_in = jnp.cumsum(cloudy) - cloudy
    weights_all = (
        embed_w,
        pos_embed,
        local_mod,
        wq,
        wk,
        wv,
        wo,
        q_gain,
        k_gain,
        out_w,
    )
    slot_ids = jnp.arange(MAXOWN, dtype=jnp.int32)
    slot_hit = (cloudy[None, :] == 1) & (order_in[None, :] == slot_ids[:, None])
    picked = jnp.sum(
        jnp.where(slot_hit, jnp.arange(tiles_here, dtype=jnp.int32)[None, :], 0), axis=1
    )
    chosen = jnp.take(tile_tokens, picked, axis=0)
    eps_chosen = denoise(chosen, *weights_all)
    eps_back = jnp.take(eps_chosen, jnp.minimum(order_in, MAXOWN - 1), axis=0)
    eps_tiles = jnp.where(cloudy[:, None, None] == 1, eps_back, jnp.zeros_like(eps_back))
    eps_latent = band_pixels(eps_tiles.astype(jnp.float32), tile_side, channels)
    cloud_cols = jnp.repeat(cloudy, band_rows) == 1
    raw_estimate = jnp.where(
        cloud_cols[None, None, :], (latent - sin_now * eps_latent) / cos_now, observed
    )
    padded = padded_2(raw_estimate, (("tile", 1),), 1)
    padded = jnp.pad(padded, ((0, 0), (0, 0), (1, 1)))
    blended = jnp.zeros_like(raw_estimate)
    for row_shift in range(3):
        for col_shift in range(3):
            window = padded[:, row_shift : row_shift + band_rows, col_shift : col_shift + band_cols]
            blended = blended + jnp.einsum(
                "oc,chw->ohw",
                conv_w[3 * row_shift + col_shift],
                window,
                precision=lax.Precision.HIGHEST,
            )
    row_pos = jnp.arange(band_rows) % band_rows
    col_pos = jnp.arange(band_cols) % band_rows
    seam_mask = ((row_pos == 0) | (row_pos == band_rows - 1))[:, None] | (
        (col_pos == 0) | (col_pos == band_rows - 1)
    )[None, :]
    estimate = jnp.where(seam_mask[None], blended, raw_estimate)
    next_latent = cos_prev * estimate + sin_prev * noise
    return (estimate, next_latent)


def solution(mesh):
    placed = (
        P(None, ("grp", "tile"), None),
        P(None, ("grp", "tile"), None),
        P(None, ("grp", "tile"), None),
        P(("grp", "tile")),
        P("grp"),
        P(),
        P(),
        P(None, "tile"),
        P("tile", None),
        P("tile", None),
        P("tile", None),
        P(None, "tile"),
        P(),
        P(),
        P(),
        P(),
    )
    return jax.shard_map(
        on_device,
        mesh=mesh,
        in_specs=placed,
        out_specs=(P(None, ("grp", "tile"), None), P(None, ("grp", "tile"), None)),
        check_vma=False,
    )
```

```python
import functools
import math

import jax
import jax.numpy as jnp
from jax import lax
from jax.experimental import pallas as pl
from jax.experimental.pallas import tpu as pltpu
from jax.sharding import PartitionSpec as P

HD = 128
PATCH = 2
MAXOWN = 3
TSTEPS = 1000
STRIDE = 20


def padded_2(block, sides, width):
    for axis, dim in sides:
        count = lax.axis_size(axis)
        forward = [(i, i + 1) for i in range(count - 1)]
        backward = [(target, source) for source, target in forward]
        low = lax.ppermute(
            lax.slice_in_dim(block, block.shape[dim] - width, None, axis=dim), axis, forward
        )
        high = lax.ppermute(lax.slice_in_dim(block, 0, width, axis=dim), axis, backward)
        block = jnp.concatenate([low, block, high], axis=dim)
    return block


def plan(step):
    theta = (step / TSTEPS + 0.008) / 1.008 * (math.pi / 2)
    return (jnp.cos(theta), jnp.sin(theta))


def time_features(step, width):
    half = width // 2
    freqs = jnp.exp(-math.log(10000.0) * jnp.arange(half, dtype=jnp.float32) / half)
    angles = step * freqs
    code = jnp.concatenate([jnp.cos(angles), jnp.sin(angles)])[None, :]
    return jax.nn.silu(code).astype(jnp.bfloat16)


def band_tiles(band, tile_side):
    channels, band_rows, band_cols = band.shape
    tiles_here = band_cols // (tile_side * PATCH)
    shaped = band.reshape(channels, tile_side, PATCH, tiles_here, tile_side, PATCH)
    return jnp.transpose(shaped, (3, 2, 5, 0, 1, 4)).reshape(
        tiles_here, PATCH * PATCH * channels, tile_side * tile_side
    )


def band_pixels(tiled, tile_side, channels):
    tiles_here = tiled.shape[0]
    shaped = tiled.reshape(tiles_here, PATCH, PATCH, channels, tile_side, tile_side)
    return jnp.transpose(shaped, (3, 4, 1, 0, 5, 2)).reshape(
        channels, tile_side * PATCH, tiles_here * tile_side * PATCH
    )


def centered(values):
    values = values.astype(jnp.float32)
    return values - jnp.mean(values, axis=-1, keepdims=True)


LO = 4


def send(src, dst, sems, slot, target):
    copy = pltpu.make_async_remote_copy(
        src_ref=src,
        dst_ref=dst,
        send_sem=sems[0].at[slot],
        recv_sem=sems[1].at[slot],
        device_id=target,
        device_id_type=pl.DeviceIdType.MESH,
    )
    copy.start()
    return copy


def pair(count):
    return [pltpu.SemaphoreType.DMA((count,)), pltpu.SemaphoreType.DMA((count,))]


def norm_rows(values):
    center = values - jnp.mean(values, axis=0, keepdims=True)
    spread = jnp.mean(center * center, axis=0, keepdims=True)
    return center, lax.rsqrt(spread + 1e-06)


def column(row):
    return jnp.broadcast_to(row, (8, row.shape[1])).T[:, 0:1]


def denoise_kernel(
    parts,
    tok_ref,
    mod_ref,
    wq_ref,
    wk_ref,
    wv_ref,
    wo_in_ref,
    emb_ref,
    pos_ref,
    out_w_ref,
    qg_ref,
    kg_ref,
    eps_ref,
    chunk_ref,
    mods_ref,
    mine_ref,
    left_ref,
    all_ref,
    wo_ref,
    h0_ref,
    mix_ref,
    flat_ref,
    flats_ref,
    shift_ref,
    ss,
    sr,
    ms,
    mr,
    cs,
    cr,
    fzs,
    fzr,
    fys,
    fyr,
    fcs,
    fcr,
    wzs,
    wzr,
    wys,
    wyr,
    wxs,
    wxr,
    wcs,
    wcr,
):
    me = lax.axis_index("tile")
    grp = lax.axis_index("grp")
    half = lax.rem(grp, 2)
    rest = 1 - half
    across = grp + 1 - 2 * half
    level, lane = me // LO, lax.rem(me, LO)
    levels = parts // LO
    side = lax.rem(lane + 2, LO)
    twin = lane + 1 - 2 * lax.rem(lane, 2)
    others = [lax.rem(me + k, parts) for k in range(1, parts)]
    line = [lax.rem(level + k, levels) * LO + lane for k in range(1, levels)]
    beside, mate = level * LO + side, level * LO + twin
    lane_slots = [lax.rem(level + levels - k, levels) * LO + lane for k in range(levels)]
    side_slots = [lax.rem(level + levels - k, levels) * LO + side for k in range(levels)]

    barrier = pltpu.get_barrier_semaphore()
    for target in others:
        pl.semaphore_signal(barrier, inc=1, device_id={"tile": target}, device_id_type=pl.DeviceIdType.MESH)
    pl.semaphore_signal(barrier, inc=1, device_id={"grp": across}, device_id_type=pl.DeviceIdType.MESH)

    per = wq_ref.shape[1] // parts
    for kind, ref in enumerate((wq_ref, wk_ref, wv_ref)):
        turned = ref[...].T
        for part in range(parts):
            chunk_ref[part, kind] = turned[part * per : (part + 1) * per]
    pl.semaphore_wait(barrier, parts)

    mod_copies = [send(mod_ref, mods_ref.at[me], (ms, mr), k, {"tile": t}) for k, t in enumerate(others)]
    chunk_copies = [send(chunk_ref.at[t], mine_ref.at[me], (cs, cr), k, {"tile": t}) for k, t in enumerate(others)]
    mods_ref[me] = mod_ref[...]
    mine_ref[me] = chunk_ref[me]
    wo_ref[me] = wo_in_ref[...]

    tiles, token_values, token_count = tok_ref.shape
    width = emb_ref.shape[1]
    pos = pos_ref[...].astype(jnp.float32)
    pos_t = pos.T
    rstds = []
    for tile in range(tiles):
        own = lax.dot_general(emb_ref[...], tok_ref[tile], (((0,), (0,)), ((), ())), preferred_element_type=jnp.float32)
        h0 = own + pos_t
        h0_ref[tile] = h0
        rstds.append(norm_rows(h0)[1])
    query_gain, key_gain = column(qg_ref[...]), column(kg_ref[...])
    for copy in mod_copies:
        copy.wait_recv()
    modulation = jnp.concatenate([mods_ref[part] for part in range(parts)], axis=1)
    scale = 1.0 + modulation[0:1, width : 2 * width]
    gate = column(modulation[:, 2 * width :])
    last = token_count + token_values
    left_ref[:token_count] = (centered(pos) * scale).astype(jnp.bfloat16)
    left_ref[token_count:last] = (centered(emb_ref[...]) * scale).astype(jnp.bfloat16)
    shift = jnp.broadcast_to(modulation[:, :width], (16, width)).astype(jnp.bfloat16)
    for copy in chunk_copies:
        copy.wait_recv()

    mine = jnp.concatenate([mine_ref[part].reshape(3 * per, -1) for part in range(parts)], axis=1)
    over_width = (((1,), (1,)), ((), ()))
    fold = lax.dot_general(mine, left_ref[...], over_width, preferred_element_type=jnp.float32)
    all_ref[me] = fold.astype(jnp.bfloat16).reshape(3, per, left_ref.shape[0])
    z_copies = [send(all_ref.at[me], all_ref.at[me], (fzs, fzr), k, {"tile": t}) for k, t in enumerate(line)]
    y_copies = [send(all_ref.at[me], all_ref.at[me], (fys, fyr), 0, {"tile": beside})]
    c_copies = [send(all_ref.at[me], all_ref.at[me], (fcs, fcr), 0, {"tile": mate})]
    flat = lax.dot_general(shift, mine, over_width, preferred_element_type=jnp.float32)[0:1]
    flat_ref[...] = jnp.zeros_like(flat_ref)
    flat_ref[:, : 3 * per] = flat
    flat_copies = [send(flat_ref, flats_ref.at[me], (ss, sr), k, {"tile": t}) for k, t in enumerate(others)]
    flats_ref[me] = flat_ref[...]
    for k, copy in enumerate(z_copies):
        copy.wait_recv()
        block = all_ref.at[lane_slots[k + 1]]
        y_copies.append(send(block, block, (fys, fyr), k + 1, {"tile": beside}))
        c_copies.append(send(block, block, (fcs, fcr), k + 1, {"tile": mate}))
    wz_copies = [
        send(wo_ref.at[me, half], wo_ref.at[me, half], (wzs, wzr), k, {"tile": t}) for k, t in enumerate(line)
    ]
    for k in range(levels):
        y_copies[k].wait_recv()
        block = all_ref.at[side_slots[k]]
        c_copies.append(send(block, block, (fcs, fcr), levels + k, {"tile": mate}))
    for copy in flat_copies:
        copy.wait_recv()
    for part in range(parts):
        shift_ref[part] = column(flats_ref[part])[: 3 * per].reshape(3, per, 1)
    wy_copies, wx_copies, wc_copies = [], [], []

    def pass_wo(copies, sems, slot, which, target):
        block = wo_ref.at[slot, which]
        copies.append(send(block, block, sems, len(copies), target))

    pass_wo(wy_copies, (wys, wyr), me, half, {"tile": beside})
    pass_wo(wc_copies, (wcs, wcr), me, half, {"tile": mate})
    pass_wo(wc_copies, (wcs, wcr), me, rest, {"tile": mate})
    for k in range(1, levels):
        wz_copies[k - 1].wait_recv()
        pass_wo(wy_copies, (wys, wyr), lane_slots[k], half, {"tile": beside})
        pass_wo(wx_copies, (wxs, wxr), lane_slots[k], half, {"grp": across})
        pass_wo(wc_copies, (wcs, wcr), lane_slots[k], half, {"tile": mate})
    for copy in c_copies:
        copy.wait_recv()

    def head_norm(proj, gain):
        spread = jnp.mean(proj * proj, axis=0, keepdims=True)
        return (proj * lax.rsqrt(spread + 1e-06) * gain).astype(jnp.bfloat16)

    group = HD // per
    heads = mix_ref.shape[1] // HD

    def attend(head):
        near = pl.ds(head * group, group)
        blocks = [all_ref[near, kind].reshape(HD, last) for kind in range(3)]
        shifts = [shift_ref[near, kind].reshape(HD, 1) for kind in range(3)]
        for tile in range(tiles):
            projs = []
            for block, base in zip(blocks, shifts):
                own = jnp.dot(block[:, token_count:last], tok_ref[tile], preferred_element_type=jnp.float32)
                proj = (own + block[:, :token_count].astype(jnp.float32)) * rstds[tile]
                projs.append(proj + base)
            query = head_norm(projs[0], query_gain)
            key = head_norm(projs[1], key_gain)
            value = projs[2].astype(jnp.bfloat16)
            scores = lax.dot_general(key, query, (((0,), (0,)), ((), ())), preferred_element_type=jnp.float32) * HD ** (-0.5)
            expo = jnp.exp(scores - jnp.max(scores, axis=0, keepdims=True))
            probs = (expo * (1.0 / jnp.sum(expo, axis=0, keepdims=True))).astype(jnp.bfloat16)
            mixed = jnp.dot(value, probs, preferred_element_type=jnp.float32)
            mix_ref[tile, pl.ds(pl.multiple_of(head * HD, HD), HD), :] = mixed.astype(jnp.bfloat16)

    pl.loop(0, heads // 4)(attend)
    for k in range(levels):
        wy_copies[k].wait_recv()
        pass_wo(wx_copies, (wxs, wxr), side_slots[k], half, {"grp": across})
        pass_wo(wc_copies, (wcs, wcr), side_slots[k], half, {"tile": mate})
    pl.loop(heads // 4, heads - heads // 4)(attend)
    for k, slot in enumerate(lane_slots[1:] + side_slots):
        wx_copies[k].wait_recv()
        pass_wo(wc_copies, (wcs, wcr), slot, rest, {"tile": mate})
    pl.loop(heads - heads // 4, heads)(attend)
    for copy in wc_copies:
        copy.wait_recv()

    wo_t = wo_ref[...].reshape(width, wo_ref.shape[3])
    for tile in range(tiles):
        attn = jnp.dot(wo_t, mix_ref[tile], preferred_element_type=jnp.float32)
        center, rstd1 = norm_rows(h0_ref[tile] + gate * attn)
        final = (center * rstd1).astype(jnp.bfloat16)
        eps = lax.dot_general(out_w_ref[...], final, (((0,), (0,)), ((), ())), preferred_element_type=jnp.float32)
        eps_ref[tile] = eps.astype(jnp.bfloat16)
    for copies in (flat_copies, mod_copies, chunk_copies, z_copies, y_copies, c_copies, wz_copies, wy_copies, wx_copies, wc_copies):
        for copy in copies:
            copy.wait_send()


def denoise(chosen, embed_w, pos_embed, local_mod, wq, wk, wv, wo, q_gain, k_gain, out_w):
    parts = lax.axis_size("tile")
    levels = parts // LO
    tiles, token_values, token_count = chosen.shape
    width = embed_w.shape[1]
    rows, inner = wq.shape
    per = inner // parts
    wo_t = wo.T.reshape(2, -1, inner)
    depth = token_count + token_values
    flat_width = -(-3 * per // HD) * HD
    args = (chosen, local_mod, wq, wk, wv, wo_t, embed_w, pos_embed, out_w, q_gain.reshape(1, -1), k_gain.reshape(1, -1))
    in_vmem = pl.BlockSpec(memory_space=pltpu.VMEM)
    bf16 = jnp.bfloat16
    return pl.pallas_call(
        functools.partial(denoise_kernel, parts),
        out_shape=jax.ShapeDtypeStruct(chosen.shape, bf16),
        in_specs=[in_vmem] * len(args),
        out_specs=in_vmem,
        scratch_shapes=[
            pltpu.VMEM((parts, 3, per, rows), bf16),
            pltpu.VMEM((parts,) + local_mod.shape, jnp.float32),
            pltpu.VMEM((parts, 3, per, rows), bf16),
            pltpu.VMEM((depth, width), bf16),
            pltpu.VMEM((parts, 3, per, depth), bf16),
            pltpu.VMEM((parts,) + wo_t.shape, bf16),
            pltpu.VMEM((tiles, width, token_count), jnp.float32),
            pltpu.VMEM((tiles, inner, token_count), bf16),
            pltpu.VMEM((1, flat_width), jnp.float32),
            pltpu.VMEM((parts, 1, flat_width), jnp.float32),
            pltpu.VMEM((parts, 3, per, 1), jnp.float32),
        ]
        + pair(parts)
        + pair(parts)
        + pair(parts)
        + pair(levels)
        + pair(levels)
        + pair(2 * levels)
        + pair(levels)
        + pair(levels)
        + pair(2 * levels)
        + pair(4 * levels),
        compiler_params=pltpu.CompilerParams(collective_id=0, has_side_effects=True, vmem_limit_bytes=60 * 1024 * 1024),
    )(*args)


def on_device(
    latent,
    observed,
    noise,
    cloudy,
    timestep,
    pos_embed,
    embed_w,
    mod_w,
    wq,
    wk,
    wv,
    wo,
    q_gain,
    k_gain,
    out_w,
    conv_w,
):
    channels, band_rows, band_cols = latent.shape
    tile_side = band_rows // PATCH
    tiles_here = band_cols // band_rows
    step_now = timestep[0].astype(jnp.float32)
    cos_now, sin_now = plan(step_now)
    cos_prev, sin_prev = plan(step_now - STRIDE)
    time_code = time_features(step_now, mod_w.shape[0])
    local_mod = jnp.dot(time_code, mod_w, preferred_element_type=jnp.float32)
    tile_tokens = band_tiles(latent.astype(jnp.bfloat16), tile_side)
    order_in = jnp.cumsum(cloudy) - cloudy
    weights_all = (
        embed_w,
        pos_embed,
        local_mod,
        wq,
        wk,
        wv,
        wo,
        q_gain,
        k_gain,
        out_w,
    )
    slot_ids = jnp.arange(MAXOWN, dtype=jnp.int32)
    slot_hit = (cloudy[None, :] == 1) & (order_in[None, :] == slot_ids[:, None])
    picked = jnp.sum(
        jnp.where(slot_hit, jnp.arange(tiles_here, dtype=jnp.int32)[None, :], 0), axis=1
    )
    chosen = jnp.take(tile_tokens, picked, axis=0)
    eps_chosen = denoise(chosen, *weights_all)
    eps_back = jnp.take(eps_chosen, jnp.minimum(order_in, MAXOWN - 1), axis=0)
    eps_tiles = jnp.where(cloudy[:, None, None] == 1, eps_back, jnp.zeros_like(eps_back))
    eps_latent = band_pixels(eps_tiles.astype(jnp.float32), tile_side, channels)
    cloud_cols = jnp.repeat(cloudy, band_rows) == 1
    raw_estimate = jnp.where(
        cloud_cols[None, None, :], (latent - sin_now * eps_latent) / cos_now, observed
    )
    padded = padded_2(raw_estimate, (("tile", 1),), 1)
    padded = jnp.pad(padded, ((0, 0), (0, 0), (1, 1)))
    blended = jnp.zeros_like(raw_estimate)
    for row_shift in range(3):
        for col_shift in range(3):
            window = padded[:, row_shift : row_shift + band_rows, col_shift : col_shift + band_cols]
            blended = blended + jnp.einsum(
                "oc,chw->ohw",
                conv_w[3 * row_shift + col_shift],
                window,
                precision=lax.Precision.HIGHEST,
            )
    row_pos = jnp.arange(band_rows) % band_rows
    col_pos = jnp.arange(band_cols) % band_rows
    seam_mask = ((row_pos == 0) | (row_pos == band_rows - 1))[:, None] | (
        (col_pos == 0) | (col_pos == band_rows - 1)
    )[None, :]
    estimate = jnp.where(seam_mask[None], blended, raw_estimate)
    next_latent = cos_prev * estimate + sin_prev * noise
    return (estimate, next_latent)


def solution(mesh):
    placed = (
        P(None, ("grp", "tile"), None),
        P(None, ("grp", "tile"), None),
        P(None, ("grp", "tile"), None),
        P(("grp", "tile")),
        P("grp"),
        P(),
        P(),
        P(None, "tile"),
        P("tile", None),
        P("tile", None),
        P("tile", None),
        P(None, "tile"),
        P(),
        P(),
        P(),
        P(),
    )
    return jax.shard_map(
        on_device,
        mesh=mesh,
        in_specs=placed,
        out_specs=(P(None, ("grp", "tile"), None), P(None, ("grp", "tile"), None)),
        check_vma=False,
    )
```

```python
import functools
import math

import jax
import jax.numpy as jnp
from jax import lax
from jax.experimental import pallas as pl
from jax.experimental.pallas import tpu as pltpu
from jax.sharding import PartitionSpec as P

HD = 128
PATCH = 2
MAXOWN = 3
TSTEPS = 1000
STRIDE = 20


def padded_2(block, sides, width):
    for axis, dim in sides:
        count = lax.axis_size(axis)
        forward = [(i, i + 1) for i in range(count - 1)]
        backward = [(target, source) for source, target in forward]
        low = lax.ppermute(
            lax.slice_in_dim(block, block.shape[dim] - width, None, axis=dim), axis, forward
        )
        high = lax.ppermute(lax.slice_in_dim(block, 0, width, axis=dim), axis, backward)
        block = jnp.concatenate([low, block, high], axis=dim)
    return block


def plan(step):
    theta = (step / TSTEPS + 0.008) / 1.008 * (math.pi / 2)
    return (jnp.cos(theta), jnp.sin(theta))


def time_features(step, width):
    half = width // 2
    freqs = jnp.exp(-math.log(10000.0) * jnp.arange(half, dtype=jnp.float32) / half)
    angles = step * freqs
    code = jnp.concatenate([jnp.cos(angles), jnp.sin(angles)])[None, :]
    return jax.nn.silu(code).astype(jnp.bfloat16)


def band_tiles(band, tile_side):
    channels, band_rows, band_cols = band.shape
    tiles_here = band_cols // (tile_side * PATCH)
    shaped = band.reshape(channels, tile_side, PATCH, tiles_here, tile_side, PATCH)
    return jnp.transpose(shaped, (3, 2, 5, 0, 1, 4)).reshape(
        tiles_here, PATCH * PATCH * channels, tile_side * tile_side
    )


def band_pixels(tiled, tile_side, channels):
    tiles_here = tiled.shape[0]
    shaped = tiled.reshape(tiles_here, PATCH, PATCH, channels, tile_side, tile_side)
    return jnp.transpose(shaped, (3, 4, 1, 0, 5, 2)).reshape(
        channels, tile_side * PATCH, tiles_here * tile_side * PATCH
    )


def centered(values):
    values = values.astype(jnp.float32)
    return values - jnp.mean(values, axis=-1, keepdims=True)


LO = 4


def send(src, dst, sems, slot, target):
    copy = pltpu.make_async_remote_copy(
        src_ref=src,
        dst_ref=dst,
        send_sem=sems[0].at[slot],
        recv_sem=sems[1].at[slot],
        device_id=target,
        device_id_type=pl.DeviceIdType.MESH,
    )
    copy.start()
    return copy


def pair(count):
    return [pltpu.SemaphoreType.DMA((count,)), pltpu.SemaphoreType.DMA((count,))]


def norm_rows(values):
    center = values - jnp.mean(values, axis=0, keepdims=True)
    spread = jnp.mean(center * center, axis=0, keepdims=True)
    return center, lax.rsqrt(spread + 1e-06)


def column(row):
    return jnp.broadcast_to(row, (8, row.shape[1])).T[:, 0:1]


def denoise_kernel(
    parts,
    tok_ref,
    mod_ref,
    wq_ref,
    wk_ref,
    wv_ref,
    wo_in_ref,
    emb_ref,
    pos_ref,
    out_w_ref,
    qg_ref,
    kg_ref,
    eps_ref,
    chunk_ref,
    mods_ref,
    mine_ref,
    left_ref,
    all_ref,
    wo_ref,
    h0_ref,
    mix_ref,
    flat_ref,
    flats_ref,
    shift_ref,
    ss,
    sr,
    ms,
    mr,
    cs,
    cr,
    fzs,
    fzr,
    fys,
    fyr,
    fcs,
    fcr,
    wzs,
    wzr,
    wys,
    wyr,
    wxs,
    wxr,
    wcs,
    wcr,
):
    me = lax.axis_index("tile")
    grp = lax.axis_index("grp")
    half = lax.rem(grp, 2)
    rest = 1 - half
    across = grp + 1 - 2 * half
    level, lane = me // LO, lax.rem(me, LO)
    levels = parts // LO
    side = lax.rem(lane + 2, LO)
    twin = lane + 1 - 2 * lax.rem(lane, 2)
    others = [lax.rem(me + k, parts) for k in range(1, parts)]
    line = [lax.rem(level + k, levels) * LO + lane for k in range(1, levels)]
    beside, mate = level * LO + side, level * LO + twin
    lane_slots = [lax.rem(level + levels - k, levels) * LO + lane for k in range(levels)]
    side_slots = [lax.rem(level + levels - k, levels) * LO + side for k in range(levels)]

    barrier = pltpu.get_barrier_semaphore()
    for target in others:
        pl.semaphore_signal(barrier, inc=1, device_id={"tile": target}, device_id_type=pl.DeviceIdType.MESH)
    pl.semaphore_signal(barrier, inc=1, device_id={"grp": across}, device_id_type=pl.DeviceIdType.MESH)

    per = wq_ref.shape[1] // parts
    for kind, ref in enumerate((wq_ref, wk_ref, wv_ref)):
        turned = ref[...].T
        for part in range(parts):
            chunk_ref[part, kind] = turned[part * per : (part + 1) * per]
    pl.semaphore_wait(barrier, parts)

    mod_copies = [send(mod_ref, mods_ref.at[me], (ms, mr), k, {"tile": t}) for k, t in enumerate(others)]
    chunk_copies = [send(chunk_ref.at[t], mine_ref.at[me], (cs, cr), k, {"tile": t}) for k, t in enumerate(others)]
    mods_ref[me] = mod_ref[...]
    mine_ref[me] = chunk_ref[me]
    wo_ref[me] = wo_in_ref[...]

    tiles, token_values, token_count = tok_ref.shape
    width = emb_ref.shape[1]
    pos = pos_ref[...].astype(jnp.float32)
    pos_t = pos.T
    rstds = []
    for tile in range(tiles):
        own = lax.dot_general(emb_ref[...], tok_ref[tile], (((0,), (0,)), ((), ())), preferred_element_type=jnp.float32)
        h0 = own + pos_t
        h0_ref[tile] = h0
        rstds.append(norm_rows(h0)[1])
    query_gain, key_gain = column(qg_ref[...]), column(kg_ref[...])
    for copy in mod_copies:
        copy.wait_recv()
    modulation = jnp.concatenate([mods_ref[part] for part in range(parts)], axis=1)
    scale = 1.0 + modulation[0:1, width : 2 * width]
    gate = column(modulation[:, 2 * width :])
    last = token_count + token_values
    left_ref[:token_count] = (centered(pos) * scale).astype(jnp.bfloat16)
    left_ref[token_count:last] = (centered(emb_ref[...]) * scale).astype(jnp.bfloat16)
    shift = jnp.broadcast_to(modulation[:, :width], (16, width)).astype(jnp.bfloat16)
    for copy in chunk_copies:
        copy.wait_recv()

    mine = jnp.concatenate([mine_ref[part].reshape(3 * per, -1) for part in range(parts)], axis=1)
    over_width = (((1,), (1,)), ((), ()))
    fold = lax.dot_general(mine, left_ref[...], over_width, preferred_element_type=jnp.float32)
    all_ref[me] = fold.astype(jnp.bfloat16).reshape(3, per, left_ref.shape[0])
    z_copies = [send(all_ref.at[me], all_ref.at[me], (fzs, fzr), k, {"tile": t}) for k, t in enumerate(line)]
    y_copies = [send(all_ref.at[me], all_ref.at[me], (fys, fyr), 0, {"tile": beside})]
    c_copies = [send(all_ref.at[me], all_ref.at[me], (fcs, fcr), 0, {"tile": mate})]
    flat = lax.dot_general(shift, mine, over_width, preferred_element_type=jnp.float32)[0:1]
    flat_ref[...] = jnp.zeros_like(flat_ref)
    flat_ref[:, : 3 * per] = flat
    flat_copies = [send(flat_ref, flats_ref.at[me], (ss, sr), k, {"tile": t}) for k, t in enumerate(others)]
    flats_ref[me] = flat_ref[...]
    for k, copy in enumerate(z_copies):
        copy.wait_recv()
        block = all_ref.at[lane_slots[k + 1]]
        y_copies.append(send(block, block, (fys, fyr), k + 1, {"tile": beside}))
        c_copies.append(send(block, block, (fcs, fcr), k + 1, {"tile": mate}))
    wz_copies = [
        send(wo_ref.at[me, half], wo_ref.at[me, half], (wzs, wzr), k, {"tile": t}) for k, t in enumerate(line)
    ]
    for k in range(levels):
        y_copies[k].wait_recv()
        block = all_ref.at[side_slots[k]]
        c_copies.append(send(block, block, (fcs, fcr), levels + k, {"tile": mate}))
    for copy in flat_copies:
        copy.wait_recv()
    for part in range(parts):
        shift_ref[part] = column(flats_ref[part])[: 3 * per].reshape(3, per, 1)
    wy_copies, wx_copies, wc_copies = [], [], []

    def pass_wo(copies, sems, slot, which, target):
        block = wo_ref.at[slot, which]
        copies.append(send(block, block, sems, len(copies), target))

    pass_wo(wy_copies, (wys, wyr), me, half, {"tile": beside})
    pass_wo(wc_copies, (wcs, wcr), me, half, {"tile": mate})
    pass_wo(wc_copies, (wcs, wcr), me, rest, {"tile": mate})
    for k in range(1, levels):
        wz_copies[k - 1].wait_recv()
        pass_wo(wy_copies, (wys, wyr), lane_slots[k], half, {"tile": beside})
        pass_wo(wx_copies, (wxs, wxr), lane_slots[k], half, {"grp": across})
        pass_wo(wc_copies, (wcs, wcr), lane_slots[k], half, {"tile": mate})
    for copy in c_copies:
        copy.wait_recv()

    def head_norm(proj, gain):
        spread = jnp.mean(proj * proj, axis=0, keepdims=True)
        return (proj * lax.rsqrt(spread + 1e-06) * gain).astype(jnp.bfloat16)

    group = HD // per
    heads = mix_ref.shape[1] // HD

    def attend(head):
        near = pl.ds(head * group, group)
        blocks = [all_ref[near, kind].reshape(HD, last) for kind in range(3)]
        shifts = [shift_ref[near, kind].reshape(HD, 1) for kind in range(3)]
        for tile in range(tiles):
            projs = []
            for block, base in zip(blocks, shifts):
                own = jnp.dot(block[:, token_count:last], tok_ref[tile], preferred_element_type=jnp.float32)
                proj = (own + block[:, :token_count].astype(jnp.float32)) * rstds[tile]
                projs.append(proj + base)
            query = head_norm(projs[0], query_gain)
            key = head_norm(projs[1], key_gain)
            value = projs[2].astype(jnp.bfloat16)
            scores = lax.dot_general(key, query, (((0,), (0,)), ((), ())), preferred_element_type=jnp.float32) * HD ** (-0.5)
            expo = jnp.exp(scores - jnp.max(scores, axis=0, keepdims=True))
            probs = (expo * (1.0 / jnp.sum(expo, axis=0, keepdims=True))).astype(jnp.bfloat16)
            mixed = jnp.dot(value, probs, preferred_element_type=jnp.float32)
            mix_ref[tile, pl.ds(pl.multiple_of(head * HD, HD), HD), :] = mixed.astype(jnp.bfloat16)

    pl.loop(0, heads // 4)(attend)
    for k in range(levels):
        wy_copies[k].wait_recv()
        pass_wo(wx_copies, (wxs, wxr), side_slots[k], half, {"grp": across})
        pass_wo(wc_copies, (wcs, wcr), side_slots[k], half, {"tile": mate})
    pl.loop(heads // 4, heads - heads // 4)(attend)
    for k, slot in enumerate(lane_slots[1:] + side_slots):
        wx_copies[k].wait_recv()
        pass_wo(wc_copies, (wcs, wcr), slot, rest, {"tile": mate})
    pl.loop(heads - heads // 4, heads)(attend)
    for copy in wc_copies:
        copy.wait_recv()

    wo_t = wo_ref[...].reshape(width, wo_ref.shape[3])
    for tile in range(tiles):
        attn = jnp.dot(wo_t, mix_ref[tile], preferred_element_type=jnp.float32)
        center, rstd1 = norm_rows(h0_ref[tile] + gate * attn)
        final = (center * rstd1).astype(jnp.bfloat16)
        eps = lax.dot_general(out_w_ref[...], final, (((0,), (0,)), ((), ())), preferred_element_type=jnp.float32)
        eps_ref[tile] = eps.astype(jnp.bfloat16)
    for copies in (flat_copies, mod_copies, chunk_copies, z_copies, y_copies, c_copies, wz_copies, wy_copies, wx_copies, wc_copies):
        for copy in copies:
            copy.wait_send()


def denoise(chosen, embed_w, pos_embed, local_mod, wq, wk, wv, wo, q_gain, k_gain, out_w):
    parts = lax.axis_size("tile")
    levels = parts // LO
    tiles, token_values, token_count = chosen.shape
    width = embed_w.shape[1]
    rows, inner = wq.shape
    per = inner // parts
    wo_t = wo.T.reshape(2, -1, inner)
    depth = token_count + token_values
    flat_width = -(-3 * per // HD) * HD
    args = (chosen, local_mod, wq, wk, wv, wo_t, embed_w, pos_embed, out_w, q_gain.reshape(1, -1), k_gain.reshape(1, -1))
    in_vmem = pl.BlockSpec(memory_space=pltpu.VMEM)
    bf16 = jnp.bfloat16
    return pl.pallas_call(
        functools.partial(denoise_kernel, parts),
        out_shape=jax.ShapeDtypeStruct(chosen.shape, bf16),
        in_specs=[in_vmem] * len(args),
        out_specs=in_vmem,
        scratch_shapes=[
            pltpu.VMEM((parts, 3, per, rows), bf16),
            pltpu.VMEM((parts,) + local_mod.shape, jnp.float32),
            pltpu.VMEM((parts, 3, per, rows), bf16),
            pltpu.VMEM((depth, width), bf16),
            pltpu.VMEM((parts, 3, per, depth), bf16),
            pltpu.VMEM((parts,) + wo_t.shape, bf16),
            pltpu.VMEM((tiles, width, token_count), jnp.float32),
            pltpu.VMEM((tiles, inner, token_count), bf16),
            pltpu.VMEM((1, flat_width), jnp.float32),
            pltpu.VMEM((parts, 1, flat_width), jnp.float32),
            pltpu.VMEM((parts, 3, per, 1), jnp.float32),
        ]
        + pair(parts)
        + pair(parts)
        + pair(parts)
        + pair(levels)
        + pair(levels)
        + pair(2 * levels)
        + pair(levels)
        + pair(levels)
        + pair(2 * levels)
        + pair(4 * levels),
        compiler_params=pltpu.CompilerParams(collective_id=0, has_side_effects=True, vmem_limit_bytes=60 * 1024 * 1024),
    )(*args)


def on_device(
    latent,
    observed,
    noise,
    cloudy,
    timestep,
    pos_embed,
    embed_w,
    mod_w,
    wq,
    wk,
    wv,
    wo,
    q_gain,
    k_gain,
    out_w,
    conv_w,
):
    channels, band_rows, band_cols = latent.shape
    tile_side = band_rows // PATCH
    tiles_here = band_cols // band_rows
    step_now = timestep[0].astype(jnp.float32)
    cos_now, sin_now = plan(step_now)
    cos_prev, sin_prev = plan(step_now - STRIDE)
    time_code = time_features(step_now, mod_w.shape[0])
    local_mod = jnp.dot(time_code, mod_w, preferred_element_type=jnp.float32)
    tile_tokens = band_tiles(latent.astype(jnp.bfloat16), tile_side)
    order_in = jnp.cumsum(cloudy) - cloudy
    weights_all = (
        embed_w,
        pos_embed,
        local_mod,
        wq,
        wk,
        wv,
        wo,
        q_gain,
        k_gain,
        out_w,
    )
    slot_ids = jnp.arange(MAXOWN, dtype=jnp.int32)
    slot_hit = (cloudy[None, :] == 1) & (order_in[None, :] == slot_ids[:, None])
    picked = jnp.sum(
        jnp.where(slot_hit, jnp.arange(tiles_here, dtype=jnp.int32)[None, :], 0), axis=1
    )
    chosen = jnp.take(tile_tokens, picked, axis=0)
    eps_chosen = denoise(chosen, *weights_all)
    eps_back = jnp.take(eps_chosen, jnp.minimum(order_in, MAXOWN - 1), axis=0)
    eps_tiles = jnp.where(cloudy[:, None, None] == 1, eps_back, jnp.zeros_like(eps_back))
    eps_latent = band_pixels(eps_tiles.astype(jnp.float32), tile_side, channels)
    cloud_cols = jnp.repeat(cloudy, band_rows) == 1
    raw_estimate = jnp.where(
        cloud_cols[None, None, :], (latent - sin_now * eps_latent) / cos_now, observed
    )
    padded = padded_2(raw_estimate, (("tile", 1),), 1)
    padded = jnp.pad(padded, ((0, 0), (0, 0), (1, 1)))
    windows = jnp.concatenate(
        [padded[:, a : a + band_rows, b : b + band_cols] for a in range(3) for b in range(3)], axis=0
    )
    taps = jnp.transpose(conv_w, (1, 0, 2)).reshape(channels, -1)
    blended = jnp.einsum("ok,khw->ohw", taps, windows, precision=lax.Precision.HIGHEST)
    row_pos = jnp.arange(band_rows) % band_rows
    col_pos = jnp.arange(band_cols) % band_rows
    seam_mask = ((row_pos == 0) | (row_pos == band_rows - 1))[:, None] | (
        (col_pos == 0) | (col_pos == band_rows - 1)
    )[None, :]
    estimate = jnp.where(seam_mask[None], blended, raw_estimate)
    next_latent = cos_prev * estimate + sin_prev * noise
    return (estimate, next_latent)


def solution(mesh):
    placed = (
        P(None, ("grp", "tile"), None),
        P(None, ("grp", "tile"), None),
        P(None, ("grp", "tile"), None),
        P(("grp", "tile")),
        P("grp"),
        P(),
        P(),
        P(None, "tile"),
        P("tile", None),
        P("tile", None),
        P("tile", None),
        P(None, "tile"),
        P(),
        P(),
        P(),
        P(),
    )
    return jax.shard_map(
        on_device,
        mesh=mesh,
        in_specs=placed,
        out_specs=(P(None, ("grp", "tile"), None), P(None, ("grp", "tile"), None)),
        check_vma=False,
    )
```
